32 devices in a mesh: row: 4 (over y, x), col: 8 (over z, core).
Axes of the slice: x: 2, y: 2, z: 4, core: 2. Of those that a mesh axis runs over, the one named last changes fastest.
Arguments:
- right_side: float32 [8, 512, 512], P('col', 'row'), may hold values from -6 to 6
- affinity_blocks: float32 [8, 8, 8, 128, 128], P('row', 'col'), may hold values from -0.046875 to 0.046875
- block_coords: int32 [8, 8, 8, 2], P('row', 'col'), may hold values from 0 to 3
- block_counts: int32 [8, 8], P('row', 'col'), may hold values from 4 to 8, as said below
Outputs:
- ranking: float32 [8, 512, 512], P('col', 'row')
- residual: float32 [8, 512, 512], P('col', 'row')
The draws below stay inside these ranges and needn't reach their ends.
Inputs may be any that keep to these rules, and one draw needn't show every extreme that they name: `block_counts`: some grid tile holds 8 live blocks in every draw.
All inputs are finite; a program needn't handle non-finite values.
Results may differ from the reference program's by a relative error of at most 0.0003.
Values sent between devices are 32-bit elements; how exact they have to be, the bound alone decides.
A program may use at most 64 MiB of HBM per device.

```python
import jax
import jax.numpy as jnp
from jax import lax

W = 512
BLK = 128
BT = 4
ITERS = 3
GRID = 8
TILE = 512
NBLK = 8


def draw_block_counts(key, part):
    lowest = (NBLK + 1) // 2
    counts = jax.random.randint(jax.random.fold_in(key, 11), (GRID * GRID,), lowest, NBLK + 1)
    chosen = jax.random.randint(jax.random.fold_in(key, 12), (), 0, GRID * GRID)
    counts = jnp.where(jnp.arange(GRID * GRID) == chosen, NBLK, counts)
    return counts.reshape(GRID, GRID).astype(jnp.int32)


def touch_ends(array, key, smallest, top_value):
    dims = array.shape
    spot = [jax.random.randint(jax.random.fold_in(key, axis), (), 0, dims[axis]) for axis in range(len(dims))]
    array = array.at[tuple(spot)].set(smallest)
    longest = dims.index(max(dims))
    spot[longest] = (spot[longest] + 1) % dims[longest]
    return array.at[tuple(spot)].set(top_value)


def block_levels(rng, extent, split, low, high):
    level, own = 1.0, jax.random.fold_in(rng, 6)
    for dim, parts in split:
        draws = jnp.exp(jax.random.uniform(jax.random.fold_in(own, dim), (parts,), jnp.float32, low / len(split), high / len(split)))
        level = level * jnp.repeat(draws, extent[dim] // parts).reshape([-1 if axis == dim else 1 for axis in range(len(extent))])
    return level


def scatter_about(key, extent, width, reach, split=(), kind=jnp.bfloat16):
    level = block_levels(key, extent, split, -0.22, 0.18) if split else 1.0
    values = jax.random.normal(key, extent, jnp.float32) * width * level
    return jnp.minimum(jnp.maximum(values, -reach), reach).astype(kind)


def setup_inputs(seed: int = 0) -> dict:
    key_of = jax.random.split(jax.random.key(seed), 5)
    return {
        "right_side": scatter_about(key_of[0], (GRID, TILE, W), 1.0, 6.0, ((0, 8), (1, 4)), jnp.float32),
        "affinity_blocks": scatter_about(key_of[1], (GRID, GRID, NBLK, BLK, BLK), (8 * GRID * NBLK * BLK // BT) ** -0.5, 0.046875, ((0, 4), (1, 8)), jnp.float32),
        "block_coords": touch_ends(jax.random.randint(key_of[2], (GRID, GRID, NBLK, 2), 0, BT), jax.random.fold_in(key_of[2], 1), 0, BT - 1).astype(jnp.int32),
        "block_counts": draw_block_counts(jax.random.fold_in(key_of[4], 71), 0),
    }


diffusion = 0.8


def live_blocks(blocks, count):
    live = (jnp.arange(blocks.shape[0], dtype=jnp.int32) < count.astype(jnp.int32)).astype(blocks.dtype)
    return blocks * live[:, None, None]


def tile_products(masked, rows, cols, column_field, row_field):
    position = jnp.arange(column_field.shape[0], dtype=jnp.int32)
    picked = jnp.take(column_field, cols.astype(jnp.int32), axis=0)
    product = jnp.einsum('kab,kbw->kaw', masked, picked, precision=lax.Precision.HIGHEST)
    row_onehot = (rows.astype(jnp.int32)[None, :] == position[:, None]).astype(masked.dtype)
    forward = jnp.einsum('tk,kaw->taw', row_onehot, product, precision=lax.Precision.HIGHEST)
    chosen = jnp.take(row_field, rows.astype(jnp.int32), axis=0)
    mirrored = jnp.einsum('kab,kaw->kbw', masked, chosen, precision=lax.Precision.HIGHEST)
    col_onehot = (cols.astype(jnp.int32)[None, :] == position[:, None]).astype(masked.dtype)
    backward = jnp.einsum('tk,kbw->tbw', col_onehot, mirrored, precision=lax.Precision.HIGHEST)
    return forward, backward


def operate(field, affinity_blocks, block_coords, block_counts):
    grid_count = field.shape[0]
    blocked = field.reshape(grid_count, BT, BLK, W)

    def visit(index, total):
        index = jnp.asarray(index).astype(jnp.int32)
        row_tile = index // grid_count
        col_tile = index % grid_count
        masked = live_blocks(affinity_blocks[row_tile, col_tile], block_counts[row_tile, col_tile])
        coords = block_coords[row_tile, col_tile]
        forward, backward = tile_products(masked, coords[:, 0], coords[:, 1], blocked[col_tile], blocked[row_tile])
        total = total.at[row_tile].add(forward)
        total = total.at[col_tile].add(backward)
        return total

    total = lax.fori_loop(0, grid_count * grid_count, visit, jnp.zeros_like(blocked))
    return field - diffusion * total.reshape(field.shape)


def reference(right_side, affinity_blocks, block_coords, block_counts):
    ranking = jnp.zeros_like(right_side)
    residual = right_side
    direction = right_side
    norm_now = jnp.sum(residual * residual, axis=(0, 1))
    for step in range(ITERS):
        image = operate(direction, affinity_blocks, block_coords, block_counts)
        alpha = norm_now / jnp.sum(direction * image, axis=(0, 1))
        ranking = ranking + alpha * direction
        residual = residual - alpha * image
        norm_next = jnp.sum(residual * residual, axis=(0, 1))
        direction = residual + (norm_next / norm_now) * direction
        norm_now = norm_next
    return ranking, residual
```

```python
import functools

import jax
import jax.numpy as jnp
from jax import lax
from jax.experimental import pallas as pl
from jax.experimental.pallas import tpu as pltpu
from jax.sharding import PartitionSpec as P

ITERS = 3
CHUNKS = 2
diffusion = 0.8
MESH = pl.DeviceIdType.MESH
f32 = jnp.float32
bf16 = jnp.bfloat16


def split(value):
    high = value.astype(bf16)
    return high, (value - high.astype(f32)).astype(bf16)


def kernel(R, PC, right, blocks, coords, counts, out_x, out_r, tile, thi, tlo, uhi, ulo, dcat,
           dz, dr, fw, fin, bw, rin, part, din, drow, drin, xs, rs,
           s0, s0s, sp1, sp1s, sb, sbs, sf, sfs, srs, srss, sd, sds, se, ses, so, sos):
    r = lax.axis_index("row")
    c = lax.axis_index("col")
    p = c // 2
    a = c % 2
    sibling = (r, 2 * p + 1 - a)
    edge = right.shape[1] * R
    sh = right.shape[1]
    cw = dz.shape[-1]
    blk = blocks.shape[-1]
    bt = edge // blk
    group = 2 * edge

    def remote(src, dst, send, recv, device):
        return pltpu.make_async_remote_copy(
            src_ref=src, dst_ref=dst, send_sem=send, recv_sem=recv, device_id=device, device_id_type=MESH)

    barrier = pltpu.get_barrier_semaphore()
    for j in range(1, R):
        pl.semaphore_signal(barrier, inc=1, device_id=(lax.rem(r + j, R), c), device_id_type=MESH)
    for j in range(1, PC):
        pl.semaphore_signal(barrier, inc=1, device_id=(r, 2 * lax.rem(p + j, PC) + a), device_id_type=MESH)
    pl.semaphore_signal(barrier, inc=1, device_id=sibling, device_id_type=MESH)
    pl.semaphore_wait(barrier, R + PC - 1)

    drain = []
    own = pl.ds(pl.multiple_of(r * sh, sh), sh)

    def columns(core, ch):
        return pl.ds(pl.multiple_of((core * CHUNKS + ch) * cw, 128), cw)

    first = []
    for ch in range(CHUNKS):
        copy = remote(right.at[0, :, columns(1 - a, ch)], dz.at[0, ch, a, own, :], s0s.at[ch], s0.at[ch], sibling)
        copy.start()
        first.append(copy)
        drain.append((None, copy))
        dz[0, ch, a, own, :] = right[0, :, columns(a, ch)]

    for m in range(2):
        @pl.loop(0, bt * bt)
        def _(q, m=m):
            t = q // bt
            u = q % bt
            total = jnp.zeros((blk, blk), f32)
            for k in range(blocks.shape[2]):
                live = (k < counts[m, 0]) & (coords[m, 0, k, 0] == t) & (coords[m, 0, k, 1] == u)
                total = total + jnp.where(live, 1.0, 0.0).astype(f32) * blocks[m, 0, k]
            tile[a, pl.ds(pl.multiple_of(m * edge + t * blk, blk), blk), pl.ds(pl.multiple_of(u * blk, blk), blk)] = total
    half = remote(tile.at[a], tile.at[a], s0s.at[CHUNKS], s0.at[CHUNKS], sibling)
    half.start()
    drain.append((None, half))

    def rows_of(s):
        return pl.ds(pl.multiple_of(s * sh, sh), sh)

    def send_p1(it, ch):
        for j in range(1, R):
            src = dz.at[it, ch, :, own, :]
            copy = remote(src, src, sp1s.at[it, ch, j], sp1.at[it, ch, j], (lax.rem(r + j, R), c))
            copy.start()
            drain.append((None, copy))

    up = (p >= r) & (p < PC - 1)
    down = (p <= r) & (p > 0)
    upper = (r, 2 * jnp.minimum(p + 1, PC - 1) + a)
    lower = (r, 2 * jnp.maximum(p - 1, 0) + a)

    def recv_wait(dst, sem):
        remote(dst, dst, sem, sem, sibling).wait_recv()

    def multiply(hi, lo, source, target):
        dh, dl = split(source)
        dcat[:, 0:cw] = dh
        dcat[:, cw:2 * cw] = dl
        step = 256
        per = edge // step

        @pl.loop(0, group // step)
        def _(i):
            rows = pl.ds(pl.multiple_of(i * step, step), step)
            wide = jnp.dot(hi[rows, :], dcat[...], preferred_element_type=f32)
            extra = jnp.dot(lo[rows, :], dcat[:, 0:cw], preferred_element_type=f32)
            target[i // per, pl.ds(pl.multiple_of((i % per) * step, step), step), :] = (
                wide[:, 0:cw] + (wide[:, cw:2 * cw] + extra))

    def fold(value):
        return jnp.sum(value.reshape(-1, 8, cw), axis=0)

    def reduce_start(n, ch, value):
        part[n, ch] = value
        for j in range(1, R):
            copy = remote(part.at[n, ch], din.at[n, ch, j], sds.at[n, ch, j], sd.at[n, ch, j], (lax.rem(r + j, R), c))
            copy.start()
            drain.append((None, copy))

    def reduce_middle(n, ch):
        total = part[n, ch]
        for j in range(1, R):
            recv_wait(din.at[n, ch, j], sd.at[n, ch, j])
            total = total + din[n, ch, j]
        drow[n, ch] = total
        for j in range(1, PC):
            copy = remote(drow.at[n, ch], drin.at[n, ch, j], ses.at[n, ch, j], se.at[n, ch, j],
                          (r, 2 * lax.rem(p + j, PC) + a))
            copy.start()
            drain.append((None, copy))

    def reduce_end(n, ch):
        total = drow[n, ch]
        for j in range(1, PC):
            recv_wait(drin.at[n, ch, j], se.at[n, ch, j])
            total = total + drin[n, ch, j]
        return total

    def column_sum(value):
        return jnp.sum(value, axis=0, keepdims=True)

    diag = p == r

    def stream(ch):
        first[ch].wait_recv()
        send_p1(0, ch)
        start = dz[0, ch, :, own, :]
        rs[ch] = start
        xs[ch] = jnp.zeros_like(start)
        reduce_start(0, ch, fold(start * start))
        yield
        reduce_middle(0, ch)
        rr = None
        for it in range(ITERS):
            for j in range(R):
                slot = lax.rem(r - j + R, R)
                if j > 0:
                    recv_wait(dz.at[it, ch, :, rows_of(slot), :], sp1.at[it, ch, j])

                @pl.when(diag)
                def _():
                    dr[it, ch, :, rows_of(slot), :] = dz[it, ch, :, rows_of(slot), :]
                    relay_now(it, ch, slot, j)
            if it == 0 and ch == 0:
                prepare()
            multiply(thi, tlo, dz[it, ch].reshape(group, cw), fw.at[it, ch])
            yield
            for j in range(R):
                slot = lax.rem(r - j + R, R)
                rows = rows_of(slot)

                @pl.when(p != r)
                def _():
                    recv_wait(dr.at[it, ch, :, rows, :], sb.at[it, ch, j])
                    relay_now(it, ch, slot, j)

                @pl.when(down)
                def _():
                    recv_wait(fin.at[it, ch, 0, :, rows, :], sf.at[it, ch, 0, j])
                    fw[it, ch, :, rows, :] += fin[it, ch, 0, :, rows, :]

                @pl.when(up)
                def _():
                    recv_wait(fin.at[it, ch, 1, :, rows, :], sf.at[it, ch, 1, j])
                    fw[it, ch, :, rows, :] += fin[it, ch, 1, :, rows, :]

                src = fw.at[it, ch, :, rows, :]
                cu = remote(src, fin.at[it, ch, 0, :, rows, :], sfs.at[it, ch, j], sf.at[it, ch, 0, j], upper)
                cd = remote(src, fin.at[it, ch, 1, :, rows, :], sfs.at[it, ch, j], sf.at[it, ch, 1, j], lower)
                pl.when(p < r)(cu.start)
                pl.when(p > r)(cd.start)
                drain.append((p < r, cu))
                drain.append((p > r, cd))
                for way, cond in ((0, up), (1, down)):
                    drain.append((cond, relay_copy(it, ch, slot, j, way)))
                yield
            multiply(uhi, ulo, dr[it, ch].reshape(group, cw), bw.at[it, ch])

            @pl.when(diag)
            def _():
                bw[it, ch] += fw[it, ch]
            for j in range(1, R):
                to = lax.rem(r + j, R)
                copy = remote(bw.at[it, ch, :, rows_of(to), :], rin.at[it, ch, j], srss.at[it, ch, j],
                              srs.at[it, ch, j], (to, c))
                copy.start()
                drain.append((None, copy))
            if it == 0:
                rr = column_sum(reduce_end(0, ch))
            yield
            total = bw[it, ch, :, own, :]
            for j in range(1, R):
                recv_wait(rin.at[it, ch, j], srs.at[it, ch, j])
                total = total + rin[it, ch, j]
            way = dz[it, ch, :, own, :]
            image = way - diffusion * total
            bw[it, ch, :, own, :] = image
            reduce_start(2 * it + 1, ch, fold(way * image))
            yield
            reduce_middle(2 * it + 1, ch)
            yield
            alpha = (rr / column_sum(reduce_end(2 * it + 1, ch)))[None]
            xs[ch] = xs[ch] + alpha * way
            residual = rs[ch] - alpha * bw[it, ch, :, own, :]
            rs[ch] = residual
            if it + 1 < ITERS:
                reduce_start(2 * it + 2, ch, fold(residual * residual))
                yield
                reduce_middle(2 * it + 2, ch)
                yield
                new = column_sum(reduce_end(2 * it + 2, ch))
                dz[it + 1, ch, :, own, :] = rs[ch] + (new / rr)[None] * dz[it, ch, :, own, :]
                rr = new
                send_p1(it + 1, ch)
                yield
        for n, (kept, out) in enumerate(((xs, out_x), (rs, out_r))):
            out[0, :, columns(a, ch)] = kept[ch, a]
            copy = remote(kept.at[ch, 1 - a], out.at[0, :, columns(a, ch)], sos.at[ch, n], so.at[ch, n], sibling)
            copy.start()
            drain.append((None, copy))
        yield
        for n in range(2):
            recv_wait(out_x.at[0, :, columns(1 - a, ch)], so.at[ch, n])

    def relay_copy(it, ch, slot, j, way):
        ref = dr.at[it, ch, :, rows_of(slot), :]
        return remote(ref, ref, sbs.at[it, ch, way, j], sb.at[it, ch, j], lower if way else upper)

    def relay_now(it, ch, slot, j):
        pl.when(up)(relay_copy(it, ch, slot, j, 0).start)
        pl.when(down)(relay_copy(it, ch, slot, j, 1).start)

    def prepare():
        half.wait_recv()

        @pl.loop(0, group // blk)
        def _(i):
            rows = pl.ds(pl.multiple_of(i * blk, blk), blk)
            for u in range(group // blk):
                piece = tile[u * blk // edge, rows, u * blk % edge:u * blk % edge + blk]
                thi[rows, u * blk:(u + 1) * blk], tlo[rows, u * blk:(u + 1) * blk] = split(piece)
                uhi[u * blk:(u + 1) * blk, rows], ulo[u * blk:(u + 1) * blk, rows] = split(piece.T)

    streams = [stream(ch) for ch in range(CHUNKS)]
    alive = list(streams)
    while alive:
        for item in list(alive):
            try:
                next(item)
            except StopIteration:
                alive.remove(item)
    for cond, copy in drain:
        if cond is None:
            copy.wait_send()
        else:
            pl.when(cond)(copy.wait_send)


def shards(R, PC, right_side, affinity_blocks, block_coords, block_counts):
    sh, W = right_side.shape[1:]
    edge = sh * R
    group = 2 * edge
    cw = W // 2 // CHUNKS
    N = 2 * ITERS
    dma = pltpu.SemaphoreType.DMA
    vm = pltpu.VMEM
    field = (ITERS, CHUNKS, 2, edge, cw)
    scratch = [
        vm((2, group, edge), f32),
        vm((group, group), bf16), vm((group, group), bf16), vm((group, group), bf16), vm((group, group), bf16),
        vm((group, 2 * cw), bf16),
        vm(field, f32), vm(field, f32), vm(field, f32),
        vm((ITERS, CHUNKS, 2, 2, edge, cw), f32),
        vm(field, f32),
        vm((ITERS, CHUNKS, R, 2, sh, cw), f32),
        vm((N, CHUNKS, 8, cw), f32), vm((N, CHUNKS, R, 8, cw), f32),
        vm((N, CHUNKS, 8, cw), f32), vm((N, CHUNKS, PC, 8, cw), f32),
        vm((CHUNKS, 2, sh, cw), f32), vm((CHUNKS, 2, sh, cw), f32),
        dma((CHUNKS + 1,)), dma((CHUNKS + 1,)),
        dma((ITERS, CHUNKS, R)), dma((ITERS, CHUNKS, R)),
        dma((ITERS, CHUNKS, R)), dma((ITERS, CHUNKS, 2, R)),
        dma((ITERS, CHUNKS, 2, R)), dma((ITERS, CHUNKS, R)),
        dma((ITERS, CHUNKS, R)), dma((ITERS, CHUNKS, R)),
        dma((N, CHUNKS, R)), dma((N, CHUNKS, R)),
        dma((N, CHUNKS, PC)), dma((N, CHUNKS, PC)),
        dma((CHUNKS, 2)), dma((CHUNKS, 2)),
    ]
    vmem = pl.BlockSpec(memory_space=pltpu.VMEM)
    smem = pl.BlockSpec(memory_space=pltpu.SMEM)
    out = jax.ShapeDtypeStruct(right_side.shape, f32)
    return pl.pallas_call(
        functools.partial(kernel, R, PC),
        out_shape=(out, out),
        in_specs=[vmem, vmem, smem, smem],
        out_specs=(vmem, vmem),
        scratch_shapes=scratch,
        compiler_params=pltpu.CompilerParams(
            collective_id=0, has_side_effects=True, vmem_limit_bytes=56 * 1024 * 1024),
    )(right_side, affinity_blocks, block_coords, block_counts)


def solution(mesh):
    in_specs = (
        P("col", "row", None),
        P("row", "col", None, None, None),
        P("row", "col", None, None),
        P("row", "col"),
    )
    out_specs = (P("col", "row", None), P("col", "row", None))
    R = mesh.shape["row"]
    PC = mesh.shape["col"] // 2
    return jax.shard_map(functools.partial(shards, R, PC), mesh=mesh, in_specs=in_specs, out_specs=out_specs, check_vma=False)
```

```python
import functools

import jax
import jax.numpy as jnp
from jax import lax
from jax.experimental import pallas as pl
from jax.experimental.pallas import tpu as pltpu
from jax.sharding import PartitionSpec as P

ITERS = 3
CHUNKS = 2
diffusion = 0.8
MESH = pl.DeviceIdType.MESH
f32 = jnp.float32
bf16 = jnp.bfloat16


def split(value):
    high = value.astype(bf16)
    return high, (value - high.astype(f32)).astype(bf16)


def kernel(R, PC, right, blocks, coords, counts, out_x, out_r, tile, thi, tlo, uhi, ulo, dcat,
           dz, dr, fw, fin, bw, rin, part, din, drow, drin, xs, rs,
           s0, s0s, sp1, sp1s, sb, sbs, sf, sfs, srs, srss, sd, sds, se, ses, so, sos):
    r = lax.axis_index("row")
    c = lax.axis_index("col")
    p = c // 2
    a = c % 2
    sibling = (r, 2 * p + 1 - a)
    edge = right.shape[1] * R
    sh = right.shape[1]
    cw = dz.shape[-1]
    blk = blocks.shape[-1]
    bt = edge // blk
    group = 2 * edge

    def remote(src, dst, send, recv, device):
        return pltpu.make_async_remote_copy(
            src_ref=src, dst_ref=dst, send_sem=send, recv_sem=recv, device_id=device, device_id_type=MESH)

    barrier = pltpu.get_barrier_semaphore()
    for j in range(1, R):
        pl.semaphore_signal(barrier, inc=1, device_id=(lax.rem(r + j, R), c), device_id_type=MESH)
    for j in range(1, PC):
        pl.semaphore_signal(barrier, inc=1, device_id=(r, 2 * lax.rem(p + j, PC) + a), device_id_type=MESH)
    pl.semaphore_signal(barrier, inc=1, device_id=sibling, device_id_type=MESH)
    pl.semaphore_wait(barrier, R + PC - 1)

    drain = []
    own = pl.ds(pl.multiple_of(r * sh, sh), sh)

    def columns(core, ch):
        return pl.ds(pl.multiple_of((core * CHUNKS + ch) * cw, 128), cw)

    first = []
    for ch in range(CHUNKS):
        copy = remote(right.at[0, :, columns(1 - a, ch)], dz.at[0, ch, a, own, :], s0s.at[ch], s0.at[ch], sibling)
        copy.start()
        first.append(copy)
        drain.append((None, copy))
        dz[0, ch, a, own, :] = right[0, :, columns(a, ch)]

    for m in range(2):
        @pl.loop(0, bt * bt)
        def _(q, m=m):
            t = q // bt
            u = q % bt
            total = jnp.zeros((blk, blk), f32)
            for k in range(blocks.shape[2]):
                live = (k < counts[m, 0]) & (coords[m, 0, k, 0] == t) & (coords[m, 0, k, 1] == u)
                total = total + jnp.where(live, 1.0, 0.0).astype(f32) * blocks[m, 0, k]
            tile[a, pl.ds(pl.multiple_of(m * edge + t * blk, blk), blk), pl.ds(pl.multiple_of(u * blk, blk), blk)] = total
    half = remote(tile.at[a], tile.at[a], s0s.at[CHUNKS], s0.at[CHUNKS], sibling)
    half.start()
    drain.append((None, half))

    def rows_of(s):
        return pl.ds(pl.multiple_of(s * sh, sh), sh)

    def send_p1(it, ch):
        for j in range(1, R):
            src = dz.at[it, ch, :, own, :]
            copy = remote(src, src, sp1s.at[it, ch, j], sp1.at[it, ch, j], (lax.rem(r + j, R), c))
            copy.start()
            drain.append((None, copy))

    up = (p >= r) & (p < PC - 1)
    down = (p <= r) & (p > 0)
    upper = (r, 2 * jnp.minimum(p + 1, PC - 1) + a)
    lower = (r, 2 * jnp.maximum(p - 1, 0) + a)

    def recv_wait(dst, sem):
        remote(dst, dst, sem, sem, sibling).wait_recv()

    def multiply(hi, lo, source, target):
        dh, dl = split(source)
        dcat[:, 0:cw] = dh
        dcat[:, cw:2 * cw] = dl
        step = 256
        per = edge // step

        @pl.loop(0, group // step)
        def _(i):
            rows = pl.ds(pl.multiple_of(i * step, step), step)
            wide = jnp.dot(hi[rows, :], dcat[...], preferred_element_type=f32)
            extra = jnp.dot(lo[rows, :], dcat[:, 0:cw], preferred_element_type=f32)
            target[i // per, pl.ds(pl.multiple_of((i % per) * step, step), step), :] = (
                wide[:, 0:cw] + (wide[:, cw:2 * cw] + extra))

    def fold(value):
        return jnp.sum(value.reshape(-1, 8, cw), axis=0)

    def reduce_start(n, ch, value):
        part[n, ch] = value
        for j in range(1, R):
            copy = remote(part.at[n, ch], din.at[n, ch, j], sds.at[n, ch, j], sd.at[n, ch, j], (lax.rem(r + j, R), c))
            copy.start()
            drain.append((None, copy))

    def reduce_middle(n, ch):
        total = part[n, ch]
        for j in range(1, R):
            recv_wait(din.at[n, ch, j], sd.at[n, ch, j])
            total = total + din[n, ch, j]
        drow[n, ch] = total
        for j in range(1, PC):
            copy = remote(drow.at[n, ch], drin.at[n, ch, j], ses.at[n, ch, j], se.at[n, ch, j],
                          (r, 2 * lax.rem(p + j, PC) + a))
            copy.start()
            drain.append((None, copy))

    def reduce_end(n, ch):
        total = drow[n, ch]
        for j in range(1, PC):
            recv_wait(drin.at[n, ch, j], se.at[n, ch, j])
            total = total + drin[n, ch, j]
        return total

    def column_sum(value):
        return jnp.sum(value, axis=0, keepdims=True)

    diag = p == r
    outermost = (p != r) & ((p == 0) | (p == PC - 1))

    def stream(ch):
        first[ch].wait_recv()
        send_p1(0, ch)
        start = dz[0, ch, :, own, :]
        rs[ch] = start
        xs[ch] = jnp.zeros_like(start)
        reduce_start(0, ch, fold(start * start))
        yield
        reduce_middle(0, ch)
        rr = None
        for it in range(ITERS):
            for j in range(R):
                slot = lax.rem(r - j + R, R)
                if j > 0:
                    recv_wait(dz.at[it, ch, :, rows_of(slot), :], sp1.at[it, ch, j])

                @pl.when(diag)
                def _():
                    dr[it, ch, :, rows_of(slot), :] = dz[it, ch, :, rows_of(slot), :]
                    relay_now(it, ch, slot, j)
            if it == 0 and ch == 0:
                prepare()
            multiply(thi, tlo, dz[it, ch].reshape(group, cw), fw.at[it, ch])
            for j in range(R):
                inward(it, ch, lax.rem(r - j + R, R), j, outermost)
            yield
            for j in range(R):
                slot = lax.rem(r - j + R, R)
                rows = rows_of(slot)

                @pl.when(p != r)
                def _():
                    recv_wait(dr.at[it, ch, :, rows, :], sb.at[it, ch, j])
                    relay_now(it, ch, slot, j)

                @pl.when(down)
                def _():
                    recv_wait(fin.at[it, ch, 0, :, rows, :], sf.at[it, ch, 0, j])
                    fw[it, ch, :, rows, :] += fin[it, ch, 0, :, rows, :]

                @pl.when(up)
                def _():
                    recv_wait(fin.at[it, ch, 1, :, rows, :], sf.at[it, ch, 1, j])
                    fw[it, ch, :, rows, :] += fin[it, ch, 1, :, rows, :]

                inward(it, ch, slot, j, jnp.logical_not(outermost))
                for way, cond in ((0, up), (1, down)):
                    drain.append((cond, relay_copy(it, ch, slot, j, way)))
                yield
            multiply(uhi, ulo, dr[it, ch].reshape(group, cw), bw.at[it, ch])

            @pl.when(diag)
            def _():
                bw[it, ch] += fw[it, ch]
            for j in range(1, R):
                to = lax.rem(r + j, R)
                copy = remote(bw.at[it, ch, :, rows_of(to), :], rin.at[it, ch, j], srss.at[it, ch, j],
                              srs.at[it, ch, j], (to, c))
                copy.start()
                drain.append((None, copy))
            if it == 0:
                rr = column_sum(reduce_end(0, ch))
            yield
            total = bw[it, ch, :, own, :]
            for j in range(1, R):
                recv_wait(rin.at[it, ch, j], srs.at[it, ch, j])
                total = total + rin[it, ch, j]
            way = dz[it, ch, :, own, :]
            image = way - diffusion * total
            bw[it, ch, :, own, :] = image
            reduce_start(2 * it + 1, ch, fold(way * image))
            yield
            reduce_middle(2 * it + 1, ch)
            yield
            alpha = (rr / column_sum(reduce_end(2 * it + 1, ch)))[None]
            xs[ch] = xs[ch] + alpha * way
            residual = rs[ch] - alpha * bw[it, ch, :, own, :]
            rs[ch] = residual
            if it + 1 < ITERS:
                reduce_start(2 * it + 2, ch, fold(residual * residual))
                yield
                reduce_middle(2 * it + 2, ch)
                yield
                new = column_sum(reduce_end(2 * it + 2, ch))
                dz[it + 1, ch, :, own, :] = rs[ch] + (new / rr)[None] * dz[it, ch, :, own, :]
                rr = new
                send_p1(it + 1, ch)
                yield
        for n, (kept, out) in enumerate(((xs, out_x), (rs, out_r))):
            out[0, :, columns(a, ch)] = kept[ch, a]
            copy = remote(kept.at[ch, 1 - a], out.at[0, :, columns(a, ch)], sos.at[ch, n], so.at[ch, n], sibling)
            copy.start()
            drain.append((None, copy))
        yield
        for n in range(2):
            recv_wait(out_x.at[0, :, columns(1 - a, ch)], so.at[ch, n])

    def inward(it, ch, slot, j, allowed):
        src = fw.at[it, ch, :, rows_of(slot), :]
        cu = remote(src, fin.at[it, ch, 0, :, rows_of(slot), :], sfs.at[it, ch, j], sf.at[it, ch, 0, j], upper)
        cd = remote(src, fin.at[it, ch, 1, :, rows_of(slot), :], sfs.at[it, ch, j], sf.at[it, ch, 1, j], lower)
        for cond, copy in (((p < r) & allowed, cu), ((p > r) & allowed, cd)):
            pl.when(cond)(copy.start)
            drain.append((cond, copy))

    def relay_copy(it, ch, slot, j, way):
        ref = dr.at[it, ch, :, rows_of(slot), :]
        return remote(ref, ref, sbs.at[it, ch, way, j], sb.at[it, ch, j], lower if way else upper)

    def relay_now(it, ch, slot, j):
        pl.when(up)(relay_copy(it, ch, slot, j, 0).start)
        pl.when(down)(relay_copy(it, ch, slot, j, 1).start)

    def prepare():
        half.wait_recv()

        @pl.loop(0, group // blk)
        def _(i):
            rows = pl.ds(pl.multiple_of(i * blk, blk), blk)
            for u in range(group // blk):
                piece = tile[u * blk // edge, rows, u * blk % edge:u * blk % edge + blk]
                thi[rows, u * blk:(u + 1) * blk], tlo[rows, u * blk:(u + 1) * blk] = split(piece)
                uhi[u * blk:(u + 1) * blk, rows], ulo[u * blk:(u + 1) * blk, rows] = split(piece.T)

    streams = [stream(ch) for ch in range(CHUNKS)]
    alive = list(streams)
    while alive:
        for item in list(alive):
            try:
                next(item)
            except StopIteration:
                alive.remove(item)
    for cond, copy in drain:
        if cond is None:
            copy.wait_send()
        else:
            pl.when(cond)(copy.wait_send)


def shards(R, PC, right_side, affinity_blocks, block_coords, block_counts):
    sh, W = right_side.shape[1:]
    edge = sh * R
    group = 2 * edge
    cw = W // 2 // CHUNKS
    N = 2 * ITERS
    dma = pltpu.SemaphoreType.DMA
    vm = pltpu.VMEM
    field = (ITERS, CHUNKS, 2, edge, cw)
    scratch = [
        vm((2, group, edge), f32),
        vm((group, group), bf16), vm((group, group), bf16), vm((group, group), bf16), vm((group, group), bf16),
        vm((group, 2 * cw), bf16),
        vm(field, f32), vm(field, f32), vm(field, f32),
        vm((ITERS, CHUNKS, 2, 2, edge, cw), f32),
        vm(field, f32),
        vm((ITERS, CHUNKS, R, 2, sh, cw), f32),
        vm((N, CHUNKS, 8, cw), f32), vm((N, CHUNKS, R, 8, cw), f32),
        vm((N, CHUNKS, 8, cw), f32), vm((N, CHUNKS, PC, 8, cw), f32),
        vm((CHUNKS, 2, sh, cw), f32), vm((CHUNKS, 2, sh, cw), f32),
        dma((CHUNKS + 1,)), dma((CHUNKS + 1,)),
        dma((ITERS, CHUNKS, R)), dma((ITERS, CHUNKS, R)),
        dma((ITERS, CHUNKS, R)), dma((ITERS, CHUNKS, 2, R)),
        dma((ITERS, CHUNKS, 2, R)), dma((ITERS, CHUNKS, R)),
        dma((ITERS, CHUNKS, R)), dma((ITERS, CHUNKS, R)),
        dma((N, CHUNKS, R)), dma((N, CHUNKS, R)),
        dma((N, CHUNKS, PC)), dma((N, CHUNKS, PC)),
        dma((CHUNKS, 2)), dma((CHUNKS, 2)),
    ]
    vmem = pl.BlockSpec(memory_space=pltpu.VMEM)
    smem = pl.BlockSpec(memory_space=pltpu.SMEM)
    out = jax.ShapeDtypeStruct(right_side.shape, f32)
    return pl.pallas_call(
        functools.partial(kernel, R, PC),
        out_shape=(out, out),
        in_specs=[vmem, vmem, smem, smem],
        out_specs=(vmem, vmem),
        scratch_shapes=scratch,
        compiler_params=pltpu.CompilerParams(
            collective_id=0, has_side_effects=True, vmem_limit_bytes=56 * 1024 * 1024),
    )(right_side, affinity_blocks, block_coords, block_counts)


def solution(mesh):
    in_specs = (
        P("col", "row", None),
        P("row", "col", None, None, None),
        P("row", "col", None, None),
        P("row", "col"),
    )
    out_specs = (P("col", "row", None), P("col", "row", None))
    R = mesh.shape["row"]
    PC = mesh.shape["col"] // 2
    return jax.shard_map(functools.partial(shards, R, PC), mesh=mesh, in_specs=in_specs, out_specs=out_specs, check_vma=False)
```

```python
import functools

import jax
import jax.numpy as jnp
from jax import lax
from jax.experimental import pallas as pl
from jax.experimental.pallas import tpu as pltpu
from jax.sharding import PartitionSpec as P

ITERS = 3
CHUNKS = 2
diffusion = 0.8
MESH = pl.DeviceIdType.MESH
f32 = jnp.float32
bf16 = jnp.bfloat16


def split(value):
    high = value.astype(bf16)
    return high, (value - high.astype(f32)).astype(bf16)


def kernel(R, PC, right, blocks, coords, counts, out_x, out_r, tile, thi, tlo, uhi, ulo, dcat,
           dz, dr, fw, fin, bw, rin, part, din, drow, drin, xs, rs,
           s0, s0s, sp1, sp1s, sb, sbs, sf, sfs, srs, srss, sd, sds, se, ses, so, sos):
    r = lax.axis_index("row")
    c = lax.axis_index("col")
    p = c // 2
    a = c % 2
    sibling = (r, 2 * p + 1 - a)
    edge = right.shape[1] * R
    sh = right.shape[1]
    cw = dz.shape[-1]
    blk = blocks.shape[-1]
    bt = edge // blk
    group = 2 * edge

    def remote(src, dst, send, recv, device):
        return pltpu.make_async_remote_copy(
            src_ref=src, dst_ref=dst, send_sem=send, recv_sem=recv, device_id=device, device_id_type=MESH)

    barrier = pltpu.get_barrier_semaphore()
    for j in range(1, R):
        pl.semaphore_signal(barrier, inc=1, device_id=(lax.rem(r + j, R), c), device_id_type=MESH)
    for j in range(1, PC):
        pl.semaphore_signal(barrier, inc=1, device_id=(r, 2 * lax.rem(p + j, PC) + a), device_id_type=MESH)
    pl.semaphore_signal(barrier, inc=1, device_id=sibling, device_id_type=MESH)
    pl.semaphore_wait(barrier, R + PC - 1)

    drain = []
    own = pl.ds(pl.multiple_of(r * sh, sh), sh)

    def columns(core, ch):
        return pl.ds(pl.multiple_of((core * CHUNKS + ch) * cw, 128), cw)

    first = []
    for ch in range(CHUNKS):
        copy = remote(right.at[0, :, columns(1 - a, ch)], dz.at[0, ch, a, own, :], s0s.at[ch], s0.at[ch], sibling)
        copy.start()
        first.append(copy)
        drain.append((None, copy))
        dz[0, ch, a, own, :] = right[0, :, columns(a, ch)]

    def rows_of(s):
        return pl.ds(pl.multiple_of(s * sh, sh), sh)

    def send_p1(it, ch):
        for j in range(1, R):
            src = dz.at[it, ch, :, own, :]
            copy = remote(src, src, sp1s.at[it, ch, j], sp1.at[it, ch, j], (lax.rem(r + j, R), c))
            copy.start()
            drain.append((None, copy))

    up = (p >= r) & (p < PC - 1)
    down = (p <= r) & (p > 0)
    upper = (r, 2 * jnp.minimum(p + 1, PC - 1) + a)
    lower = (r, 2 * jnp.maximum(p - 1, 0) + a)

    def recv_wait(dst, sem):
        remote(dst, dst, sem, sem, sibling).wait_recv()

    def multiply(hi, lo, source, target):
        dh, dl = split(source)
        dcat[:, 0:cw] = dh
        dcat[:, cw:2 * cw] = dl
        step = 256
        per = edge // step

        @pl.loop(0, group // step)
        def _(i):
            rows = pl.ds(pl.multiple_of(i * step, step), step)
            wide = jnp.dot(hi[rows, :], dcat[...], preferred_element_type=f32)
            extra = jnp.dot(lo[rows, :], dcat[:, 0:cw], preferred_element_type=f32)
            target[i // per, pl.ds(pl.multiple_of((i % per) * step, step), step), :] = (
                wide[:, 0:cw] + (wide[:, cw:2 * cw] + extra))

    def fold(value):
        return jnp.sum(value.reshape(-1, 8, cw), axis=0)

    def reduce_start(n, ch, value):
        part[n, ch] = value
        for j in range(1, R):
            copy = remote(part.at[n, ch], din.at[n, ch, j], sds.at[n, ch, j], sd.at[n, ch, j], (lax.rem(r + j, R), c))
            copy.start()
            drain.append((None, copy))

    def reduce_middle(n, ch):
        total = part[n, ch]
        for j in range(1, R):
            recv_wait(din.at[n, ch, j], sd.at[n, ch, j])
            total = total + din[n, ch, j]
        drow[n, ch] = total
        for j in range(1, PC):
            copy = remote(drow.at[n, ch], drin.at[n, ch, j], ses.at[n, ch, j], se.at[n, ch, j],
                          (r, 2 * lax.rem(p + j, PC) + a))
            copy.start()
            drain.append((None, copy))

    def reduce_end(n, ch):
        total = drow[n, ch]
        for j in range(1, PC):
            recv_wait(drin.at[n, ch, j], se.at[n, ch, j])
            total = total + drin[n, ch, j]
        return total

    def column_sum(value):
        return jnp.sum(value, axis=0, keepdims=True)

    diag = p == r
    outermost = (p != r) & ((p == 0) | (p == PC - 1))

    def stream(ch):
        first[ch].wait_recv()
        send_p1(0, ch)
        start = dz[0, ch, :, own, :]
        rs[ch] = start
        xs[ch] = jnp.zeros_like(start)
        reduce_start(0, ch, fold(start * start))
        yield
        reduce_middle(0, ch)
        rr = None
        for it in range(ITERS):
            for j in range(R):
                slot = lax.rem(r - j + R, R)
                if j > 0:
                    recv_wait(dz.at[it, ch, :, rows_of(slot), :], sp1.at[it, ch, j])

                @pl.when(diag)
                def _():
                    dr[it, ch, :, rows_of(slot), :] = dz[it, ch, :, rows_of(slot), :]
                    relay_now(it, ch, slot, j)
            if it == 0 and ch == 0:
                prepare()
            multiply(thi, tlo, dz[it, ch].reshape(group, cw), fw.at[it, ch])
            for j in range(R):
                inward(it, ch, lax.rem(r - j + R, R), j, outermost)
            yield
            for tick in range(R + 1):
                if tick < R:
                    pl.when(near)(functools.partial(outward_step, it, ch, tick))
                    pl.when(far)(functools.partial(inward_step, it, ch, tick))
                if tick > 0:
                    pl.when(near)(functools.partial(inward_step, it, ch, tick - 1))
                    pl.when(far)(functools.partial(outward_step, it, ch, tick - 1))
                yield
            for j in range(R):
                slot = lax.rem(r - j + R, R)
                for way, cond in ((0, up), (1, down)):
                    drain.append((cond, relay_copy(it, ch, slot, j, way)))
                for way, cond in ((0, p < r), (1, p > r)):
                    drain.append((cond, inward_copy(it, ch, slot, j, way)))
            multiply(uhi, ulo, dr[it, ch].reshape(group, cw), bw.at[it, ch])

            @pl.when(diag)
            def _():
                bw[it, ch] += fw[it, ch]
            for j in range(1, R):
                to = lax.rem(r + j, R)
                copy = remote(bw.at[it, ch, :, rows_of(to), :], rin.at[it, ch, j], srss.at[it, ch, j],
                              srs.at[it, ch, j], (to, c))
                copy.start()
                drain.append((None, copy))
            if it == 0:
                rr = column_sum(reduce_end(0, ch))
            yield
            total = bw[it, ch, :, own, :]
            for j in range(1, R):
                recv_wait(rin.at[it, ch, j], srs.at[it, ch, j])
                total = total + rin[it, ch, j]
            way = dz[it, ch, :, own, :]
            image = way - diffusion * total
            bw[it, ch, :, own, :] = image
            reduce_start(2 * it + 1, ch, fold(way * image))
            yield
            reduce_middle(2 * it + 1, ch)
            yield
            alpha = (rr / column_sum(reduce_end(2 * it + 1, ch)))[None]
            xs[ch] = xs[ch] + alpha * way
            residual = rs[ch] - alpha * bw[it, ch, :, own, :]
            rs[ch] = residual
            if it + 1 < ITERS:
                reduce_start(2 * it + 2, ch, fold(residual * residual))
                yield
                reduce_middle(2 * it + 2, ch)
                yield
                new = column_sum(reduce_end(2 * it + 2, ch))
                dz[it + 1, ch, :, own, :] = rs[ch] + (new / rr)[None] * dz[it, ch, :, own, :]
                rr = new
                send_p1(it + 1, ch)
                yield
        for n, (kept, out) in enumerate(((xs, out_x), (rs, out_r))):
            out[0, :, columns(a, ch)] = kept[ch, a]
            copy = remote(kept.at[ch, 1 - a], out.at[0, :, columns(a, ch)], sos.at[ch, n], so.at[ch, n], sibling)
            copy.start()
            drain.append((None, copy))
        yield
        for n in range(2):
            recv_wait(out_x.at[0, :, columns(1 - a, ch)], so.at[ch, n])

    near = jnp.abs(p - r) <= 1
    far = jnp.abs(p - r) > 1

    def outward_step(it, ch, j):
        slot = lax.rem(r - j + R, R)

        @pl.when(p != r)
        def _():
            recv_wait(dr.at[it, ch, :, rows_of(slot), :], sb.at[it, ch, j])
            relay_now(it, ch, slot, j)

    def inward_step(it, ch, j):
        slot = lax.rem(r - j + R, R)
        rows = rows_of(slot)
        for way, cond in ((0, down), (1, up)):
            @pl.when(cond)
            def _():
                recv_wait(fin.at[it, ch, way, :, rows, :], sf.at[it, ch, way, j])
                fw[it, ch, :, rows, :] += fin[it, ch, way, :, rows, :]
        inward(it, ch, slot, j, jnp.logical_not(outermost))

    def inward_copy(it, ch, slot, j, way):
        src = fw.at[it, ch, :, rows_of(slot), :]
        return remote(src, fin.at[it, ch, way, :, rows_of(slot), :], sfs.at[it, ch, j], sf.at[it, ch, way, j],
                      lower if way else upper)

    def inward(it, ch, slot, j, allowed):
        pl.when((p < r) & allowed)(inward_copy(it, ch, slot, j, 0).start)
        pl.when((p > r) & allowed)(inward_copy(it, ch, slot, j, 1).start)

    def relay_copy(it, ch, slot, j, way):
        ref = dr.at[it, ch, :, rows_of(slot), :]
        return remote(ref, ref, sbs.at[it, ch, way, j], sb.at[it, ch, j], lower if way else upper)

    def relay_now(it, ch, slot, j):
        pl.when(up)(relay_copy(it, ch, slot, j, 0).start)
        pl.when(down)(relay_copy(it, ch, slot, j, 1).start)

    def prepare():
        half.wait_recv()

        @pl.loop(0, group // blk)
        def _(i):
            rows = pl.ds(pl.multiple_of(i * blk, blk), blk)
            for u in range(group // blk):
                piece = tile[u * blk // edge, rows, u * blk % edge:u * blk % edge + blk]
                thi[rows, u * blk:(u + 1) * blk], tlo[rows, u * blk:(u + 1) * blk] = split(piece)
                uhi[u * blk:(u + 1) * blk, rows], ulo[u * blk:(u + 1) * blk, rows] = split(piece.T)

    streams = [stream(ch) for ch in range(CHUNKS)]
    for item in streams:
        next(item)
    for m in range(2):
        @pl.loop(0, bt * bt)
        def _(q, m=m):
            t = q // bt
            u = q % bt
            total = jnp.zeros((blk, blk), f32)
            for k in range(blocks.shape[2]):
                live = (k < counts[m, 0]) & (coords[m, 0, k, 0] == t) & (coords[m, 0, k, 1] == u)
                total = total + jnp.where(live, 1.0, 0.0).astype(f32) * blocks[m, 0, k]
            tile[a, pl.ds(pl.multiple_of(m * edge + t * blk, blk), blk), pl.ds(pl.multiple_of(u * blk, blk), blk)] = total
    half = remote(tile.at[a], tile.at[a], s0s.at[CHUNKS], s0.at[CHUNKS], sibling)
    half.start()
    drain.append((None, half))
    alive = list(streams)
    while alive:
        for item in list(alive):
            try:
                next(item)
            except StopIteration:
                alive.remove(item)
    for cond, copy in drain:
        if cond is None:
            copy.wait_send()
        else:
            pl.when(cond)(copy.wait_send)


def shards(R, PC, right_side, affinity_blocks, block_coords, block_counts):
    sh, W = right_side.shape[1:]
    edge = sh * R
    group = 2 * edge
    cw = W // 2 // CHUNKS
    N = 2 * ITERS
    dma = pltpu.SemaphoreType.DMA
    vm = pltpu.VMEM
    field = (ITERS, CHUNKS, 2, edge, cw)
    scratch = [
        vm((2, group, edge), f32),
        vm((group, group), bf16), vm((group, group), bf16), vm((group, group), bf16), vm((group, group), bf16),
        vm((group, 2 * cw), bf16),
        vm(field, f32), vm(field, f32), vm(field, f32),
        vm((ITERS, CHUNKS, 2, 2, edge, cw), f32),
        vm(field, f32),
        vm((ITERS, CHUNKS, R, 2, sh, cw), f32),
        vm((N, CHUNKS, 8, cw), f32), vm((N, CHUNKS, R, 8, cw), f32),
        vm((N, CHUNKS, 8, cw), f32), vm((N, CHUNKS, PC, 8, cw), f32),
        vm((CHUNKS, 2, sh, cw), f32), vm((CHUNKS, 2, sh, cw), f32),
        dma((CHUNKS + 1,)), dma((CHUNKS + 1,)),
        dma((ITERS, CHUNKS, R)), dma((ITERS, CHUNKS, R)),
        dma((ITERS, CHUNKS, R)), dma((ITERS, CHUNKS, 2, R)),
        dma((ITERS, CHUNKS, 2, R)), dma((ITERS, CHUNKS, R)),
        dma((ITERS, CHUNKS, R)), dma((ITERS, CHUNKS, R)),
        dma((N, CHUNKS, R)), dma((N, CHUNKS, R)),
        dma((N, CHUNKS, PC)), dma((N, CHUNKS, PC)),
        dma((CHUNKS, 2)), dma((CHUNKS, 2)),
    ]
    vmem = pl.BlockSpec(memory_space=pltpu.VMEM)
    smem = pl.BlockSpec(memory_space=pltpu.SMEM)
    out = jax.ShapeDtypeStruct(right_side.shape, f32)
    return pl.pallas_call(
        functools.partial(kernel, R, PC),
        out_shape=(out, out),
        in_specs=[vmem, vmem, smem, smem],
        out_specs=(vmem, vmem),
        scratch_shapes=scratch,
        compiler_params=pltpu.CompilerParams(
            collective_id=0, has_side_effects=True, vmem_limit_bytes=56 * 1024 * 1024),
    )(right_side, affinity_blocks, block_coords, block_counts)


def solution(mesh):
    in_specs = (
        P("col", "row", None),
        P("row", "col", None, None, None),
        P("row", "col", None, None),
        P("row", "col"),
    )
    out_specs = (P("col", "row", None), P("col", "row", None))
    R = mesh.shape["row"]
    PC = mesh.shape["col"] // 2
    return jax.shard_map(functools.partial(shards, R, PC), mesh=mesh, in_specs=in_specs, out_specs=out_specs, check_vma=False)
```

```python
import functools

import jax
import jax.numpy as jnp
from jax import lax
from jax.experimental import pallas as pl
from jax.experimental.pallas import tpu as pltpu
from jax.sharding import PartitionSpec as P

ITERS = 3
CHUNKS = 2
LEAD = 3
diffusion = 0.8
MESH = pl.DeviceIdType.MESH
f32 = jnp.float32
bf16 = jnp.bfloat16


def split(value):
    high = value.astype(bf16)
    return high, (value - high.astype(f32)).astype(bf16)


def kernel(R, PC, right, blocks, coords, counts, out_x, out_r, tile, thi, tlo, uhi, ulo, dcat,
           dz, dr, fw, fin, bw, rin, part, din, drow, drin, xs, rs, ds, im,
           s0, s0s, sp1, sp1s, sb, sbs, sf, sfs, srs, srss, sd, sds, se, ses, so, sos):
    r = lax.axis_index("row")
    c = lax.axis_index("col")
    p = c // 2
    a = c % 2
    sibling = (r, 2 * p + 1 - a)
    edge = right.shape[1] * R
    sh = right.shape[1]
    cw = dz.shape[-1]
    blk = blocks.shape[-1]
    bt = edge // blk
    group = 2 * edge

    def remote(src, dst, send, recv, device):
        return pltpu.make_async_remote_copy(
            src_ref=src, dst_ref=dst, send_sem=send, recv_sem=recv, device_id=device, device_id_type=MESH)

    barrier = pltpu.get_barrier_semaphore()
    for j in range(1, R):
        pl.semaphore_signal(barrier, inc=1, device_id=(lax.rem(r + j, R), c), device_id_type=MESH)
    for j in range(1, PC):
        pl.semaphore_signal(barrier, inc=1, device_id=(r, 2 * lax.rem(p + j, PC) + a), device_id_type=MESH)
    pl.semaphore_signal(barrier, inc=1, device_id=sibling, device_id_type=MESH)
    pl.semaphore_wait(barrier, R + PC - 1)

    drain = []
    own = pl.ds(pl.multiple_of(r * sh, sh), sh)

    def columns(core, ch):
        return pl.ds(pl.multiple_of((core * CHUNKS + ch) * cw, 128), cw)

    first = []
    for ch in range(CHUNKS):
        copy = remote(right.at[0, :, columns(1 - a, ch)], dz.at[0, ch, a, own, :], s0s.at[ch], s0.at[ch], sibling)
        copy.start()
        first.append(copy)
        drain.append((None, copy))
        dz[0, ch, a, own, :] = right[0, :, columns(a, ch)]

    def rows_of(s):
        return pl.ds(pl.multiple_of(s * sh, sh), sh)

    def send_p1(it, ch):
        for j in range(1, R):
            src = dz.at[it, ch, :, own, :]
            copy = remote(src, src, sp1s.at[it, ch, j], sp1.at[it, ch, j], (lax.rem(r + j, R), c))
            copy.start()
            drain.append((None, copy))

    up = (p >= r) & (p < PC - 1)
    down = (p <= r) & (p > 0)
    upper = (r, 2 * jnp.minimum(p + 1, PC - 1) + a)
    lower = (r, 2 * jnp.maximum(p - 1, 0) + a)

    def recv_wait(dst, sem):
        remote(dst, dst, sem, sem, sibling).wait_recv()

    def multiply(hi, lo, source, target):
        dh, dl = split(source)
        dcat[:, 0:cw] = dh
        dcat[:, cw:2 * cw] = dl
        step = 256
        per = edge // step

        @pl.loop(0, group // step)
        def _(i):
            rows = pl.ds(pl.multiple_of(i * step, step), step)
            wide = jnp.dot(hi[rows, :], dcat[...], preferred_element_type=f32)
            extra = jnp.dot(lo[rows, :], dcat[:, 0:cw], preferred_element_type=f32)
            target[i // per, pl.ds(pl.multiple_of((i % per) * step, step), step), :] = (
                wide[:, 0:cw] + (wide[:, cw:2 * cw] + extra))

    def fold(value):
        return jnp.sum(value.reshape(-1, 8, cw), axis=0)

    def reduce_start(n, ch, value):
        part[n, ch] = value
        for j in range(1, R):
            copy = remote(part.at[n, ch], din.at[n, ch, j], sds.at[n, ch, j], sd.at[n, ch, j], (lax.rem(r + j, R), c))
            copy.start()
            drain.append((None, copy))

    def reduce_middle(n, ch):
        total = part[n, ch]
        for j in range(1, R):
            recv_wait(din.at[n, ch, j], sd.at[n, ch, j])
            total = total + din[n, ch, j]
        drow[n, ch] = total
        for j in range(1, PC):
            copy = remote(drow.at[n, ch], drin.at[n, ch, j], ses.at[n, ch, j], se.at[n, ch, j],
                          (r, 2 * lax.rem(p + j, PC) + a))
            copy.start()
            drain.append((None, copy))

    def reduce_end(n, ch):
        total = drow[n, ch]
        for j in range(1, PC):
            recv_wait(drin.at[n, ch, j], se.at[n, ch, j])
            total = total + drin[n, ch, j]
        return total

    def column_sum(value):
        return jnp.sum(value, axis=0, keepdims=True)

    diag = p == r
    outermost = (p != r) & ((p == 0) | (p == PC - 1))

    def stream(ch):
        first[ch].wait_recv()
        start = dz[0, ch, :, own, :]
        xs[ch] = jnp.zeros_like(start)
        reduce_start(0, ch, fold(start * start))
        send_p1(0, ch)
        yield
        rr = None
        for it in range(ITERS):
            for j in range(R):
                slot = lax.rem(r - j + R, R)
                if j > 0:
                    recv_wait(dz.at[it, ch, :, rows_of(slot), :], sp1.at[it, ch, j])

                @pl.when(diag)
                def _():
                    dr[it, ch, :, rows_of(slot), :] = dz[it, ch, :, rows_of(slot), :]
                    relay_now(it, ch, slot, j)
            if it == 0 and ch == 0:
                prepare()
            multiply(thi, tlo, dz[it, ch].reshape(group, cw), fw.at[it, ch])
            for j in range(R):
                inward(it, ch, lax.rem(r - j + R, R), j, outermost)
            reduce_middle(2 * it, ch)
            yield
            for tick in range(R + 1):
                if tick < R:
                    pl.when(near)(functools.partial(outward_step, it, ch, tick))
                    pl.when(far)(functools.partial(inward_step, it, ch, tick))
                if tick > 0:
                    pl.when(near)(functools.partial(inward_step, it, ch, tick - 1))
                    pl.when(far)(functools.partial(outward_step, it, ch, tick - 1))
                yield
            for j in range(R):
                slot = lax.rem(r - j + R, R)
                for way, cond in ((0, up), (1, down)):
                    drain.append((cond, relay_copy(it, ch, slot, j, way)))
                for way, cond in ((0, p < r), (1, p > r)):
                    drain.append((cond, inward_copy(it, ch, slot, j, way)))
            multiply(uhi, ulo, dr[it, ch].reshape(group, cw), bw.at[it, ch])

            @pl.when(diag)
            def _():
                bw[it, ch] += fw[it, ch]
            for j in range(1, R):
                to = lax.rem(r + j, R)
                copy = remote(bw.at[it, ch, :, rows_of(to), :], rin.at[it, ch, j], srss.at[it, ch, j],
                              srs.at[it, ch, j], (to, c))
                copy.start()
                drain.append((None, copy))
            yield
            total = bw[it, ch, :, own, :]
            for j in range(1, R):
                recv_wait(rin.at[it, ch, j], srs.at[it, ch, j])
                total = total + rin[it, ch, j]
            way = dz[it, ch, :, own, :]
            image = way - diffusion * total
            norm = column_sum(reduce_end(2 * it, ch))
            if it > 0:
                beta = (norm / rr)[None]
                way = way + beta * ds[ch]
                image = image + beta * im[ch]
            rr = norm
            ds[ch] = way
            im[ch] = image
            reduce_start(2 * it + 1, ch, fold(way * image))
            yield
            reduce_middle(2 * it + 1, ch)
            yield
            alpha = (rr / column_sum(reduce_end(2 * it + 1, ch)))[None]
            residual = dz[it, ch, :, own, :] - alpha * im[ch]
            if it + 1 < ITERS:
                dz[it + 1, ch, :, own, :] = residual
                reduce_start(2 * it + 2, ch, fold(residual * residual))
                send_p1(it + 1, ch)
            else:
                rs[ch] = residual
            xs[ch] = xs[ch] + alpha * ds[ch]
            if it + 1 < ITERS:
                yield
        for n, (kept, out) in enumerate(((xs, out_x), (rs, out_r))):
            out[0, :, columns(a, ch)] = kept[ch, a]
            copy = remote(kept.at[ch, 1 - a], out.at[0, :, columns(a, ch)], sos.at[ch, n], so.at[ch, n], sibling)
            copy.start()
            drain.append((None, copy))
        yield
        for n in range(2):
            recv_wait(out_x.at[0, :, columns(1 - a, ch)], so.at[ch, n])

    near = jnp.abs(p - r) <= 1
    far = jnp.abs(p - r) > 1

    def outward_step(it, ch, j):
        slot = lax.rem(r - j + R, R)

        @pl.when(p != r)
        def _():
            recv_wait(dr.at[it, ch, :, rows_of(slot), :], sb.at[it, ch, j])
            relay_now(it, ch, slot, j)

    def inward_step(it, ch, j):
        slot = lax.rem(r - j + R, R)
        rows = rows_of(slot)
        for way, cond in ((0, down), (1, up)):
            @pl.when(cond)
            def _():
                recv_wait(fin.at[it, ch, way, :, rows, :], sf.at[it, ch, way, j])
                fw[it, ch, :, rows, :] += fin[it, ch, way, :, rows, :]
        inward(it, ch, slot, j, jnp.logical_not(outermost))

    def inward_copy(it, ch, slot, j, way):
        src = fw.at[it, ch, :, rows_of(slot), :]
        return remote(src, fin.at[it, ch, way, :, rows_of(slot), :], sfs.at[it, ch, j], sf.at[it, ch, way, j],
                      lower if way else upper)

    def inward(it, ch, slot, j, allowed):
        pl.when((p < r) & allowed)(inward_copy(it, ch, slot, j, 0).start)
        pl.when((p > r) & allowed)(inward_copy(it, ch, slot, j, 1).start)

    def relay_copy(it, ch, slot, j, way):
        ref = dr.at[it, ch, :, rows_of(slot), :]
        return remote(ref, ref, sbs.at[it, ch, way, j], sb.at[it, ch, j], lower if way else upper)

    def relay_now(it, ch, slot, j):
        pl.when(up)(relay_copy(it, ch, slot, j, 0).start)
        pl.when(down)(relay_copy(it, ch, slot, j, 1).start)

    def prepare():
        half.wait_recv()

        @pl.loop(0, group // blk)
        def _(i):
            rows = pl.ds(pl.multiple_of(i * blk, blk), blk)
            for u in range(group // blk):
                piece = tile[u * blk // edge, rows, u * blk % edge:u * blk % edge + blk]
                thi[rows, u * blk:(u + 1) * blk], tlo[rows, u * blk:(u + 1) * blk] = split(piece)
                uhi[u * blk:(u + 1) * blk, rows], ulo[u * blk:(u + 1) * blk, rows] = split(piece.T)

    streams = [stream(ch) for ch in range(CHUNKS)]
    for item in streams:
        next(item)
    for m in range(2):
        @pl.loop(0, bt * bt)
        def _(q, m=m):
            t = q // bt
            u = q % bt
            total = jnp.zeros((blk, blk), f32)
            for k in range(blocks.shape[2]):
                live = (k < counts[m, 0]) & (coords[m, 0, k, 0] == t) & (coords[m, 0, k, 1] == u)
                total = total + jnp.where(live, 1.0, 0.0).astype(f32) * blocks[m, 0, k]
            tile[a, pl.ds(pl.multiple_of(m * edge + t * blk, blk), blk), pl.ds(pl.multiple_of(u * blk, blk), blk)] = total
    half = remote(tile.at[a], tile.at[a], s0s.at[CHUNKS], s0.at[CHUNKS], sibling)
    half.start()
    drain.append((None, half))
    alive = list(streams)
    for _ in range(LEAD):
        next(streams[0])
    while alive:
        for item in list(alive):
            try:
                next(item)
            except StopIteration:
                alive.remove(item)
    for cond, copy in drain:
        if cond is None:
            copy.wait_send()
        else:
            pl.when(cond)(copy.wait_send)


def shards(R, PC, right_side, affinity_blocks, block_coords, block_counts):
    sh, W = right_side.shape[1:]
    edge = sh * R
    group = 2 * edge
    cw = W // 2 // CHUNKS
    N = 2 * ITERS
    dma = pltpu.SemaphoreType.DMA
    vm = pltpu.VMEM
    field = (ITERS, CHUNKS, 2, edge, cw)
    scratch = [
        vm((2, group, edge), f32),
        vm((group, group), bf16), vm((group, group), bf16), vm((group, group), bf16), vm((group, group), bf16),
        vm((group, 2 * cw), bf16),
        vm(field, f32), vm(field, f32), vm(field, f32),
        vm((ITERS, CHUNKS, 2, 2, edge, cw), f32),
        vm(field, f32),
        vm((ITERS, CHUNKS, R, 2, sh, cw), f32),
        vm((N, CHUNKS, 8, cw), f32), vm((N, CHUNKS, R, 8, cw), f32),
        vm((N, CHUNKS, 8, cw), f32), vm((N, CHUNKS, PC, 8, cw), f32),
        vm((CHUNKS, 2, sh, cw), f32), vm((CHUNKS, 2, sh, cw), f32),
        vm((CHUNKS, 2, sh, cw), f32), vm((CHUNKS, 2, sh, cw), f32),
        dma((CHUNKS + 1,)), dma((CHUNKS + 1,)),
        dma((ITERS, CHUNKS, R)), dma((ITERS, CHUNKS, R)),
        dma((ITERS, CHUNKS, R)), dma((ITERS, CHUNKS, 2, R)),
        dma((ITERS, CHUNKS, 2, R)), dma((ITERS, CHUNKS, R)),
        dma((ITERS, CHUNKS, R)), dma((ITERS, CHUNKS, R)),
        dma((N, CHUNKS, R)), dma((N, CHUNKS, R)),
        dma((N, CHUNKS, PC)), dma((N, CHUNKS, PC)),
        dma((CHUNKS, 2)), dma((CHUNKS, 2)),
    ]
    vmem = pl.BlockSpec(memory_space=pltpu.VMEM)
    smem = pl.BlockSpec(memory_space=pltpu.SMEM)
    out = jax.ShapeDtypeStruct(right_side.shape, f32)
    return pl.pallas_call(
        functools.partial(kernel, R, PC),
        out_shape=(out, out),
        in_specs=[vmem, vmem, smem, smem],
        out_specs=(vmem, vmem),
        scratch_shapes=scratch,
        compiler_params=pltpu.CompilerParams(
            collective_id=0, has_side_effects=True, vmem_limit_bytes=56 * 1024 * 1024),
    )(right_side, affinity_blocks, block_coords, block_counts)


def solution(mesh):
    in_specs = (
        P("col", "row", None),
        P("row", "col", None, None, None),
        P("row", "col", None, None),
        P("row", "col"),
    )
    out_specs = (P("col", "row", None), P("col", "row", None))
    R = mesh.shape["row"]
    PC = mesh.shape["col"] // 2
    return jax.shard_map(functools.partial(shards, R, PC), mesh=mesh, in_specs=in_specs, out_specs=out_specs, check_vma=False)
```

```python
import functools

import jax
import jax.numpy as jnp
from jax import lax
from jax.experimental import pallas as pl
from jax.experimental.pallas import tpu as pltpu
from jax.sharding import PartitionSpec as P

ITERS = 3
CHUNKS = 2
LEAD = 0
diffusion = 0.8
MESH = pl.DeviceIdType.MESH
f32 = jnp.float32
bf16 = jnp.bfloat16


def split(value):
    high = value.astype(bf16)
    return high, (value - high.astype(f32)).astype(bf16)


def kernel(R, PC, right, blocks, coords, counts, out_x, out_r, tile, thi, tlo, uhi, ulo, dcat,
           dz, dr, fw, fin, bw, rin, part, din, drow, drin, xs, rs, ds, im,
           s0, s0s, sp1, sp1s, sb, sbs, sf, sfs, srs, srss, sd, sds, se, ses, so, sos):
    r = lax.axis_index("row")
    c = lax.axis_index("col")
    p = c // 2
    a = c % 2
    sibling = (r, 2 * p + 1 - a)
    edge = right.shape[1] * R
    sh = right.shape[1]
    cw = dz.shape[-1]
    blk = blocks.shape[-1]
    bt = edge // blk
    group = 2 * edge

    def remote(src, dst, send, recv, device):
        return pltpu.make_async_remote_copy(
            src_ref=src, dst_ref=dst, send_sem=send, recv_sem=recv, device_id=device, device_id_type=MESH)

    barrier = pltpu.get_barrier_semaphore()
    for j in range(1, R):
        pl.semaphore_signal(barrier, inc=1, device_id=(lax.rem(r + j, R), c), device_id_type=MESH)
    for j in range(1, PC):
        pl.semaphore_signal(barrier, inc=1, device_id=(r, 2 * lax.rem(p + j, PC) + a), device_id_type=MESH)
    pl.semaphore_signal(barrier, inc=1, device_id=sibling, device_id_type=MESH)
    pl.semaphore_wait(barrier, R + PC - 1)

    drain = []
    own = pl.ds(pl.multiple_of(r * sh, sh), sh)

    def columns(core, ch):
        return pl.ds(pl.multiple_of((core * CHUNKS + ch) * cw, 128), cw)

    first = []
    for ch in range(CHUNKS):
        copy = remote(right.at[0, :, columns(1 - a, ch)], dz.at[0, ch, a, own, :], s0s.at[ch], s0.at[ch], sibling)
        copy.start()
        first.append(copy)
        drain.append((None, copy))
        dz[0, ch, a, own, :] = right[0, :, columns(a, ch)]

    def rows_of(s):
        return pl.ds(pl.multiple_of(s * sh, sh), sh)

    def send_p1(it, ch):
        for j in range(1, R):
            src = dz.at[it, ch, :, own, :]
            copy = remote(src, src, sp1s.at[it, ch, j], sp1.at[it, ch, j], (lax.rem(r + j, R), c))
            copy.start()
            drain.append((None, copy))

    up = (p >= r) & (p < PC - 1)
    down = (p <= r) & (p > 0)
    upper = (r, 2 * jnp.minimum(p + 1, PC - 1) + a)
    lower = (r, 2 * jnp.maximum(p - 1, 0) + a)

    def recv_wait(dst, sem):
        remote(dst, dst, sem, sem, sibling).wait_recv()

    def multiply(hi, lo, source, target):
        dh, dl = split(source)
        dcat[:, 0:cw] = dh
        dcat[:, cw:2 * cw] = dl
        step = 256
        per = edge // step

        @pl.loop(0, group // step)
        def _(i):
            rows = pl.ds(pl.multiple_of(i * step, step), step)
            wide = jnp.dot(hi[rows, :], dcat[...], preferred_element_type=f32)
            extra = jnp.dot(lo[rows, :], dcat[:, 0:cw], preferred_element_type=f32)
            target[i // per, pl.ds(pl.multiple_of((i % per) * step, step), step), :] = (
                wide[:, 0:cw] + (wide[:, cw:2 * cw] + extra))

    def fold(value):
        return jnp.sum(value.reshape(-1, 8, cw), axis=0)

    def reduce_start(n, ch, value):
        part[n, ch] = value
        for j in range(1, R):
            copy = remote(part.at[n, ch], din.at[n, ch, j], sds.at[n, ch, j], sd.at[n, ch, j], (lax.rem(r + j, R), c))
            copy.start()
            drain.append((None, copy))

    def reduce_middle(n, ch):
        total = part[n, ch]
        for j in range(1, R):
            recv_wait(din.at[n, ch, j], sd.at[n, ch, j])
            total = total + din[n, ch, j]
        drow[n, ch] = total
        for j in range(1, PC):
            copy = remote(drow.at[n, ch], drin.at[n, ch, j], ses.at[n, ch, j], se.at[n, ch, j],
                          (r, 2 * lax.rem(p + j, PC) + a))
            copy.start()
            drain.append((None, copy))

    def reduce_end(n, ch):
        total = drow[n, ch]
        for j in range(1, PC):
            recv_wait(drin.at[n, ch, j], se.at[n, ch, j])
            total = total + drin[n, ch, j]
        return total

    def column_sum(value):
        return jnp.sum(value, axis=0, keepdims=True)

    diag = p == r
    outermost = (p != r) & ((p == 0) | (p == PC - 1))

    def stream(ch):
        first[ch].wait_recv()
        start = dz[0, ch, :, own, :]
        xs[ch] = jnp.zeros_like(start)
        reduce_start(0, ch, fold(start * start))
        send_p1(0, ch)
        yield
        rr = None
        for it in range(ITERS):
            for j in range(R):
                slot = lax.rem(r - j + R, R)
                if j > 0:
                    recv_wait(dz.at[it, ch, :, rows_of(slot), :], sp1.at[it, ch, j])

                @pl.when(diag)
                def _():
                    dr[it, ch, :, rows_of(slot), :] = dz[it, ch, :, rows_of(slot), :]
                    relay_now(it, ch, slot, j)
            if it == 0 and ch == 0:
                prepare()
            multiply(thi, tlo, dz[it, ch].reshape(group, cw), fw.at[it, ch])
            for j in range(R):
                inward(it, ch, lax.rem(r - j + R, R), j, outermost)
            reduce_middle(2 * it, ch)
            yield
            for tick in range(R + 1):
                if tick < R:
                    pl.when(near)(functools.partial(outward_step, it, ch, tick))
                    pl.when(far)(functools.partial(inward_step, it, ch, tick))
                if tick > 0:
                    pl.when(near)(functools.partial(inward_step, it, ch, tick - 1))
                    pl.when(far)(functools.partial(outward_step, it, ch, tick - 1))
                if it == 0 and ch == CHUNKS - 1 and tick < R:
                    transpose_part(tick)
                yield
            for j in range(R):
                slot = lax.rem(r - j + R, R)
                for way, cond in ((0, up), (1, down)):
                    drain.append((cond, relay_copy(it, ch, slot, j, way)))
                for way, cond in ((0, p < r), (1, p > r)):
                    drain.append((cond, inward_copy(it, ch, slot, j, way)))
            multiply(uhi, ulo, dr[it, ch].reshape(group, cw), bw.at[it, ch])

            @pl.when(diag)
            def _():
                bw[it, ch] += fw[it, ch]
            for j in range(1, R):
                to = lax.rem(r + j, R)
                copy = remote(bw.at[it, ch, :, rows_of(to), :], rin.at[it, ch, j], srss.at[it, ch, j],
                              srs.at[it, ch, j], (to, c))
                copy.start()
                drain.append((None, copy))
            yield
            total = bw[it, ch, :, own, :]
            for j in range(1, R):
                recv_wait(rin.at[it, ch, j], srs.at[it, ch, j])
                total = total + rin[it, ch, j]
            way = dz[it, ch, :, own, :]
            image = way - diffusion * total
            norm = column_sum(reduce_end(2 * it, ch))
            if it > 0:
                beta = (norm / rr)[None]
                way = way + beta * ds[ch]
                image = image + beta * im[ch]
            rr = norm
            ds[ch] = way
            im[ch] = image
            reduce_start(2 * it + 1, ch, fold(way * image))
            yield
            reduce_middle(2 * it + 1, ch)
            yield
            alpha = (rr / column_sum(reduce_end(2 * it + 1, ch)))[None]
            residual = dz[it, ch, :, own, :] - alpha * im[ch]
            if it + 1 < ITERS:
                dz[it + 1, ch, :, own, :] = residual
                reduce_start(2 * it + 2, ch, fold(residual * residual))
                send_p1(it + 1, ch)
            else:
                rs[ch] = residual
            xs[ch] = xs[ch] + alpha * ds[ch]
            if it + 1 < ITERS:
                yield
        for n, (kept, out) in enumerate(((xs, out_x), (rs, out_r))):
            out[0, :, columns(a, ch)] = kept[ch, a]
            copy = remote(kept.at[ch, 1 - a], out.at[0, :, columns(a, ch)], sos.at[ch, n], so.at[ch, n], sibling)
            copy.start()
            drain.append((None, copy))
        yield
        for n in range(2):
            recv_wait(out_x.at[0, :, columns(1 - a, ch)], so.at[ch, n])

    near = jnp.abs(p - r) <= 1
    far = jnp.abs(p - r) > 1

    def outward_step(it, ch, j):
        slot = lax.rem(r - j + R, R)

        @pl.when(p != r)
        def _():
            recv_wait(dr.at[it, ch, :, rows_of(slot), :], sb.at[it, ch, j])
            relay_now(it, ch, slot, j)

    def inward_step(it, ch, j):
        slot = lax.rem(r - j + R, R)
        rows = rows_of(slot)
        for way, cond in ((0, down), (1, up)):
            @pl.when(cond)
            def _():
                recv_wait(fin.at[it, ch, way, :, rows, :], sf.at[it, ch, way, j])
                fw[it, ch, :, rows, :] += fin[it, ch, way, :, rows, :]
        inward(it, ch, slot, j, jnp.logical_not(outermost))

    def inward_copy(it, ch, slot, j, way):
        src = fw.at[it, ch, :, rows_of(slot), :]
        return remote(src, fin.at[it, ch, way, :, rows_of(slot), :], sfs.at[it, ch, j], sf.at[it, ch, way, j],
                      lower if way else upper)

    def inward(it, ch, slot, j, allowed):
        pl.when((p < r) & allowed)(inward_copy(it, ch, slot, j, 0).start)
        pl.when((p > r) & allowed)(inward_copy(it, ch, slot, j, 1).start)

    def relay_copy(it, ch, slot, j, way):
        ref = dr.at[it, ch, :, rows_of(slot), :]
        return remote(ref, ref, sbs.at[it, ch, way, j], sb.at[it, ch, j], lower if way else upper)

    def relay_now(it, ch, slot, j):
        pl.when(up)(relay_copy(it, ch, slot, j, 0).start)
        pl.when(down)(relay_copy(it, ch, slot, j, 1).start)

    def split_half(core):
        @pl.loop(0, group // blk)
        def _(i):
            rows = pl.ds(pl.multiple_of(i * blk, blk), blk)
            cols = pl.ds(pl.multiple_of(core * edge, edge), edge)
            thi[rows, cols], tlo[rows, cols] = split(tile[core, rows, :])

    def prepare():
        split_half(a)
        for copy in halves:
            copy.wait_recv()
        split_half(1 - a)

    def transpose_part(tick):
        count = group // blk // R

        @pl.loop(tick * count, (tick + 1) * count)
        def _(i):
            rows = pl.ds(pl.multiple_of(i * blk, blk), blk)
            for u in range(group // blk):
                piece = tile[u * blk // edge, rows, u * blk % edge:u * blk % edge + blk]
                uhi[u * blk:(u + 1) * blk, rows], ulo[u * blk:(u + 1) * blk, rows] = split(piece.T)

    streams = [stream(ch) for ch in range(CHUNKS)]
    for item in streams:
        next(item)
    halves = []
    for m in range(2):
        @pl.loop(0, bt * bt)
        def _(q, m=m):
            t = q // bt
            u = q % bt
            total = jnp.zeros((blk, blk), f32)
            for k in range(blocks.shape[2]):
                live = (k < counts[m, 0]) & (coords[m, 0, k, 0] == t) & (coords[m, 0, k, 1] == u)
                total = total + jnp.where(live, 1.0, 0.0).astype(f32) * blocks[m, 0, k]
            tile[a, pl.ds(pl.multiple_of(m * edge + t * blk, blk), blk), pl.ds(pl.multiple_of(u * blk, blk), blk)] = total
        band = tile.at[a, pl.ds(m * edge, edge), :]
        copy = remote(band, band, s0s.at[CHUNKS + m], s0.at[CHUNKS + m], sibling)
        copy.start()
        halves.append(copy)
        drain.append((None, copy))
    alive = list(streams)
    for _ in range(LEAD):
        next(streams[0])
    while alive:
        for item in list(alive):
            try:
                next(item)
            except StopIteration:
                alive.remove(item)
    for cond, copy in drain:
        if cond is None:
            copy.wait_send()
        else:
            pl.when(cond)(copy.wait_send)


def shards(R, PC, right_side, affinity_blocks, block_coords, block_counts):
    sh, W = right_side.shape[1:]
    edge = sh * R
    group = 2 * edge
    cw = W // 2 // CHUNKS
    N = 2 * ITERS
    dma = pltpu.SemaphoreType.DMA
    vm = pltpu.VMEM
    field = (ITERS, CHUNKS, 2, edge, cw)
    scratch = [
        vm((2, group, edge), f32),
        vm((group, group), bf16), vm((group, group), bf16), vm((group, group), bf16), vm((group, group), bf16),
        vm((group, 2 * cw), bf16),
        vm(field, f32), vm(field, f32), vm(field, f32),
        vm((ITERS, CHUNKS, 2, 2, edge, cw), f32),
        vm(field, f32),
        vm((ITERS, CHUNKS, R, 2, sh, cw), f32),
        vm((N, CHUNKS, 8, cw), f32), vm((N, CHUNKS, R, 8, cw), f32),
        vm((N, CHUNKS, 8, cw), f32), vm((N, CHUNKS, PC, 8, cw), f32),
        vm((CHUNKS, 2, sh, cw), f32), vm((CHUNKS, 2, sh, cw), f32),
        vm((CHUNKS, 2, sh, cw), f32), vm((CHUNKS, 2, sh, cw), f32),
        dma((CHUNKS + 2,)), dma((CHUNKS + 2,)),
        dma((ITERS, CHUNKS, R)), dma((ITERS, CHUNKS, R)),
        dma((ITERS, CHUNKS, R)), dma((ITERS, CHUNKS, 2, R)),
        dma((ITERS, CHUNKS, 2, R)), dma((ITERS, CHUNKS, R)),
        dma((ITERS, CHUNKS, R)), dma((ITERS, CHUNKS, R)),
        dma((N, CHUNKS, R)), dma((N, CHUNKS, R)),
        dma((N, CHUNKS, PC)), dma((N, CHUNKS, PC)),
        dma((CHUNKS, 2)), dma((CHUNKS, 2)),
    ]
    vmem = pl.BlockSpec(memory_space=pltpu.VMEM)
    smem = pl.BlockSpec(memory_space=pltpu.SMEM)
    out = jax.ShapeDtypeStruct(right_side.shape, f32)
    return pl.pallas_call(
        functools.partial(kernel, R, PC),
        out_shape=(out, out),
        in_specs=[vmem, vmem, smem, smem],
        out_specs=(vmem, vmem),
        scratch_shapes=scratch,
        compiler_params=pltpu.CompilerParams(
            collective_id=0, has_side_effects=True, vmem_limit_bytes=56 * 1024 * 1024),
    )(right_side, affinity_blocks, block_coords, block_counts)


def solution(mesh):
    in_specs = (
        P("col", "row", None),
        P("row", "col", None, None, None),
        P("row", "col", None, None),
        P("row", "col"),
    )
    out_specs = (P("col", "row", None), P("col", "row", None))
    R = mesh.shape["row"]
    PC = mesh.shape["col"] // 2
    return jax.shard_map(functools.partial(shards, R, PC), mesh=mesh, in_specs=in_specs, out_specs=out_specs, check_vma=False)
```
